512 devices in a mesh: grp: 16 (over z, core), aux: 32 (over x, y).
Axes of the slice: x: 4, y: 8, z: 8, core: 2. Of those that a mesh axis runs over, the one named last changes fastest.
Arguments:
- integrals: bfloat16 [2048, 262144], P('aux', 'grp'), parts along dimension 1, may hold values from -6 to 6
- inverses: bfloat16 [4, 512, 512], P(None, 'aux'), as said below
- lower_blocks: bfloat16 [6, 512, 512], P(None, 'aux'), may hold values from -0.25 to 0.25
Outputs:
- solved: bfloat16 [2048, 262144], P(None, ('grp', 'aux')), parts along dimension 1
The draws below stay inside these ranges and needn't reach their ends.
There are 16 independent parts, one for each index of `grp`. The reference program is written for one: setup_inputs(seed, part) draws one part's arguments, and reference() takes and returns one part's arrays. A program takes and returns all parts, laid end to end along the dimension named above; an argument that names none is the same for every part. Nothing has to cross between parts.
Inputs may be any that keep to these rules, and one draw needn't show every extreme that they name: Each inverses[k] is lower triangular with diagonal entries between 0.5 and 1.5.
All inputs are finite; a program needn't handle non-finite values.
Results may differ from the reference program's by a relative error of at most 0.007.
Values may be sent and summed in bfloat16 or wider, within the bound.
No kernel may reach another device: no remote copies, remote signals or barrier semaphores. Data moves between devices by JAX's collectives and lax.ppermute only.
A program may use at most 64 MiB of HBM per device.

```python
import jax
import jax.numpy as jnp

PANEL = 512
PANELS = 4
NAUXW = 2048
NBLOCKS = 6
ROWS = 16384


def draw_inverses(key, part):
    key_off = jax.random.fold_in(key, 11)
    key_diag = jax.random.fold_in(key, 12)
    shape = (PANELS, PANEL, PANEL)
    offdiag = jax.random.normal(key_off, shape, jnp.float32) * (1.5 * PANEL ** (-0.5))
    diag_vals = jax.random.uniform(key_diag, shape, jnp.float32, 0.5, 1.5)
    row_ids = jax.lax.broadcasted_iota(jnp.int32, shape, 1)
    col_ids = jax.lax.broadcasted_iota(jnp.int32, shape, 2)
    result = jnp.where(row_ids > col_ids, offdiag, 0.0) + jnp.where(row_ids == col_ids, diag_vals, 0.0)
    return result.astype(jnp.bfloat16)


def levels(own_key, shape, split, least, high):
    def one(axis_at, blocks):
        steps = jax.random.uniform(jax.random.fold_in(jax.random.fold_in(own_key, 6), axis_at), (blocks,), jnp.float32, least / len(split), high / len(split))
        return jnp.repeat(jnp.exp(steps), shape[axis_at] // blocks).reshape((-1,) + (1,) * (len(shape) - axis_at - 1))

    level = one(*split[0])
    for cut in split[1:]:
        level = level * one(*cut)
    return level


def bell_draw(own_key, dims, spread, most, shards=(), kind=jnp.bfloat16):
    drawn = spread * jax.random.normal(own_key, dims, jnp.float32)
    if shards:
        drawn = drawn * levels(own_key, dims, shards, -0.22, 0.18)
    return jnp.clip(drawn, -most, most).astype(kind)


def setup_inputs(seed: int = 0, part: int = 0) -> dict:
    key_list = jax.random.split(jax.random.key(seed), 4)
    part_splits = jax.random.split(jax.random.fold_in(key_list[3], part), 4)
    return {
        "integrals": bell_draw(part_splits[0], (NAUXW, ROWS), 1.0, 6.0, ((0, 32),)),
        "inverses": draw_inverses(jax.random.fold_in(key_list[3], 71), part),
        "lower_blocks": bell_draw(key_list[2], (NBLOCKS, PANEL, PANEL), PANEL ** -0.5, 0.25, ((1, 32),)),
    }


def reference(integrals, inverses, lower_blocks):
    outs = []
    for k in range(PANELS):
        acc = integrals[k * PANEL:(k + 1) * PANEL, :].astype(jnp.float32)
        for j in range(k):
            acc = acc - jnp.dot(lower_blocks[k * (k - 1) // 2 + j], outs[j], preferred_element_type=jnp.float32)
        rest = acc.astype(jnp.bfloat16)
        outs.append(jnp.dot(inverses[k], rest, preferred_element_type=jnp.float32).astype(jnp.bfloat16))
    return jnp.concatenate(outs, axis=0)
```

```python
import functools

import jax
import jax.numpy as jnp
from jax import lax
from jax.experimental import pallas as pl
from jax.experimental.pallas import tpu as pltpu
from jax.sharding import Mesh, PartitionSpec as P

NX, NY = 4, 8
EARLY = 128
ANY = pl.BlockSpec(memory_space=pl.ANY)
VMEM = pl.BlockSpec(memory_space=pltpu.VMEM)


def run_all(copies):
    for copy in copies:
        copy.start()
    for copy in copies:
        copy.wait()


def pack_first(integrals, inverses, lower_blocks, first, sems):
    x, core = lax.axis_index("x"), lax.axis_index("core")
    width = integrals.shape[2] // (NX * NY)
    copies = []
    for y in range(NY):
        for s in range(NX):
            at = pl.multiple_of(lax.rem(x + s, NX) * (NY * width) + y * width, 128)
            copies.append(
                pltpu.make_async_copy(
                    integrals.at[:, :, pl.ds(at, EARLY)],
                    first.at[y, 0:4, :, s * EARLY : (s + 1) * EARLY],
                    sems.at[len(copies)],
                )
            )
    count = len(copies)
    for copy in copies:
        copy.start()

    @pl.when(core == 0)
    def _():
        mine = []
        for y in range(NY):
            mine.append(
                pltpu.make_async_copy(inverses, first.at[y, 4:8], sems.at[count + 2 * y])
            )
            mine.append(
                pltpu.make_async_copy(
                    lower_blocks.at[0:1], first.at[y, 8:9], sems.at[count + 2 * y + 1]
                )
            )
        run_all(mine)

    @pl.when(core == 1)
    def _():
        run_all(
            [
                pltpu.make_async_copy(
                    lower_blocks.at[1:6], first.at[y, 4:9], sems.at[count + 2 * y]
                )
                for y in range(NY)
            ]
        )

    for copy in copies:
        copy.wait()


def pack_late(integrals, s0, s1, s2, s3, sems):
    x = lax.axis_index("x")
    width = integrals.shape[1] // (NX * NY)
    copies = []
    for s, slab in ((1, s1), (3, s3), (2, s2), (0, s0)):
        for y in range(NY):
            at = pl.multiple_of(
                lax.rem(x + s, NX) * (NY * width) + y * width + EARLY, 128
            )
            copies.append(
                pltpu.make_async_copy(
                    integrals.at[:, pl.ds(at, width - EARLY)],
                    slab.at[y],
                    sems.at[len(copies)],
                )
            )
    run_all(copies)


def assemble(*refs):
    own, other, early = refs[0:4], refs[4:8], refs[8:12]
    factor, columns, sems = refs[12:]
    x, core = lax.axis_index("x"), lax.axis_index("core")
    copies = []
    for s in range(NX):
        source = lax.rem(x + NX - s, NX)
        for pieces, half in ((own, core), (other, 1 - core)):
            for y in range(NY):
                row = pl.multiple_of(source * 128 + y * 16, 16)
                copies.append(
                    pltpu.make_async_copy(
                        pieces[s].at[y],
                        factor.at[half, :, pl.ds(row, 16), :],
                        sems.at[len(copies)],
                    )
                )
        copies.append(
            pltpu.make_async_copy(early[s], columns.at[source], sems.at[len(copies)])
        )
    run_all(copies)


def solve(factor, early, late, out, held, sems):
    x = lax.axis_index("x")
    solved = []
    copies = []
    for k in range(4):
        slot = lax.rem(x + NX - k, NX)
        acc = jnp.concatenate(
            [
                early[k].reshape(512, EARLY),
                late[:, slot].reshape(512, 512 - EARLY),
            ],
            axis=1,
        ).astype(jnp.float32)
        for j in range(k):
            acc = acc - jnp.dot(
                factor[4 + k * (k - 1) // 2 + j],
                held[j],
                preferred_element_type=jnp.float32,
            )
        held[k] = jnp.dot(
            factor[k], acc.astype(jnp.bfloat16), preferred_element_type=jnp.float32
        ).astype(jnp.bfloat16)
        copies.append(
            pltpu.make_async_copy(
                held.at[k], out.at[k * 512 : (k + 1) * 512], sems.at[k]
            )
        )
        copies[-1].start()
    for copy in copies:
        copy.wait()


def cost(flops, moved):
    return pl.CostEstimate(flops=flops, bytes_accessed=moved, transcendentals=0)


def ring(count, shift):
    return [(i, (i + shift) % count) for i in range(count)]


def local(integrals, inverses, lower_blocks):
    rows, total = integrals.shape
    width = total // (NX * NY)
    bf16 = jnp.bfloat16
    late_width = width - EARLY

    first = pl.pallas_call(
        pack_first,
        out_shape=jax.ShapeDtypeStruct((NY, 9, 16, width), bf16),
        in_specs=[ANY] * 3,
        out_specs=ANY,
        scratch_shapes=[pltpu.SemaphoreType.DMA((NX * NY + 2 * NY,))],
        cost_estimate=cost(0, 3 << 20),
    )(integrals.reshape(4, 16, total), inverses, lower_blocks)
    first = lax.all_to_all(first, "y", 0, 0, tiled=True)

    slabs = pl.pallas_call(
        pack_late,
        out_shape=[jax.ShapeDtypeStruct((NY, rows, late_width), bf16)] * NX,
        in_specs=[ANY],
        out_specs=[ANY] * NX,
        scratch_shapes=[pltpu.SemaphoreType.DMA((NX * NY,))],
        cost_estimate=cost(0, 3 << 20),
    )(integrals)
    moved = {0: slabs[0]}
    for s in (1, 3, 2):
        moved[s] = lax.ppermute(slabs[s], "x", ring(NX, s))
    late = jnp.stack([moved[s] for s in range(NX)], axis=1)
    late = lax.all_to_all(late, "y", 0, 0, tiled=True)

    own = {0: first[:, 4:9]}
    for s in (1, 3, 2):
        own[s] = lax.ppermute(own[0], "x", ring(NX, s))
    other = {s: lax.ppermute(own[s], "core", ring(2, 1)) for s in range(NX)}
    early = {
        s: first[:, 0:4, :, s * EARLY : (s + 1) * EARLY] for s in range(NX)
    }
    for s in (1, 3, 2):
        early[s] = lax.ppermute(early[s], "x", ring(NX, s))

    factor, columns = pl.pallas_call(
        assemble,
        out_shape=[
            jax.ShapeDtypeStruct((2, 5, 512, 512), bf16),
            jax.ShapeDtypeStruct((NX, NY, 4, 16, EARLY), bf16),
        ],
        in_specs=[ANY] * (3 * NX),
        out_specs=[ANY] * 2,
        scratch_shapes=[pltpu.SemaphoreType.DMA((NX * (2 * NY + 1),))],
        cost_estimate=cost(0, 11 << 20),
    )(*[d[s] for d in (own, other, early) for s in range(NX)])

    return pl.pallas_call(
        solve,
        out_shape=jax.ShapeDtypeStruct((4 * 512, width), bf16),
        in_specs=[VMEM] * 3,
        out_specs=ANY,
        scratch_shapes=[
            pltpu.VMEM((4, 512, width), bf16),
            pltpu.SemaphoreType.DMA((4,)),
        ],
        compiler_params=pltpu.CompilerParams(vmem_limit_bytes=32 << 20),
        cost_estimate=cost(20 * 512**3, 9 << 20),
    )(factor.reshape(10, 512, 512), columns, late)


def solution(mesh):
    fine = Mesh(mesh.devices.reshape(8, 2, NX, NY), ("z", "core", "x", "y"))
    aux, grp = ("x", "y"), ("z", "core")
    placed = (P(aux, grp), P(None, aux, None), P(None, aux, None))
    return jax.shard_map(
        local,
        mesh=fine,
        in_specs=placed,
        out_specs=P(None, grp + aux),
        check_vma=False,
    )
```

```python
import functools

import jax
import jax.numpy as jnp
from jax import lax
from jax.experimental import pallas as pl
from jax.experimental.pallas import tpu as pltpu
from jax.sharding import Mesh, PartitionSpec as P

NX, NY = 4, 8
EARLY = 128
ANY = pl.BlockSpec(memory_space=pl.ANY)
VMEM = pl.BlockSpec(memory_space=pltpu.VMEM)


def run_all(copies):
    for copy in copies:
        copy.start()
    for copy in copies:
        copy.wait()


def pack_first(integrals, inverses, lower_blocks, first, sems):
    x, core = lax.axis_index("x"), lax.axis_index("core")
    width = integrals.shape[2] // (NX * NY)
    copies = []
    for y in range(NY):
        for s in range(NX):
            at = pl.multiple_of(lax.rem(x + s, NX) * (NY * width) + y * width, 128)
            copies.append(
                pltpu.make_async_copy(
                    integrals.at[:, :, pl.ds(at, EARLY)],
                    first.at[y, 0:4, :, s * EARLY : (s + 1) * EARLY],
                    sems.at[len(copies)],
                )
            )
    count = len(copies)
    for copy in copies:
        copy.start()

    @pl.when(core == 0)
    def _():
        mine = []
        for y in range(NY):
            mine.append(
                pltpu.make_async_copy(inverses, first.at[y, 4:8], sems.at[count + 2 * y])
            )
            mine.append(
                pltpu.make_async_copy(
                    lower_blocks.at[0:1], first.at[y, 8:9], sems.at[count + 2 * y + 1]
                )
            )
        run_all(mine)

    @pl.when(core == 1)
    def _():
        run_all(
            [
                pltpu.make_async_copy(
                    lower_blocks.at[1:6], first.at[y, 4:9], sems.at[count + 2 * y]
                )
                for y in range(NY)
            ]
        )

    for copy in copies:
        copy.wait()


def pack_late(integrals, s0, s1, s2, s3, sems):
    x = lax.axis_index("x")
    width = integrals.shape[1] // (NX * NY)
    copies = []
    for s, slab in ((1, s1), (3, s3), (2, s2), (0, s0)):
        for y in range(NY):
            at = pl.multiple_of(
                lax.rem(x + s, NX) * (NY * width) + y * width + EARLY, 128
            )
            copies.append(
                pltpu.make_async_copy(
                    integrals.at[:, pl.ds(at, width - EARLY)],
                    slab.at[y],
                    sems.at[len(copies)],
                )
            )
    run_all(copies)


def assemble(*refs):
    own, other, early = refs[0:4], refs[4:8], refs[8:12]
    factor, columns = refs[12:]
    x, core = lax.axis_index("x"), lax.axis_index("core")
    for s in range(NX):
        source = lax.rem(x + NX - s, NX)
        columns[source] = early[s][...]
        row = pl.multiple_of(source * 128, 128)
        for pieces, half in ((own, core), (other, 1 - core)):
            for b in range(5):
                factor[half, b, pl.ds(row, 128), :] = pieces[s][:, b].reshape(128, 512)


def solve(factor, early, late, out, panels, held, sems):
    x = lax.axis_index("x")
    order = [b for k in range(4) for b in [4 + k * (k - 1) // 2 + j for j in range(k)] + [k]]
    loads = {
        b: pltpu.make_async_copy(factor.at[b], panels.at[b], sems.at[b]) for b in order
    }
    for b in order:
        loads[b].start()
    stores = []
    for k in range(4):
        slot = lax.rem(x + NX - k, NX)
        acc = jnp.concatenate(
            [
                early[k].reshape(512, EARLY),
                late[:, slot].reshape(512, 512 - EARLY),
            ],
            axis=1,
        ).astype(jnp.float32)
        for j in range(k):
            b = 4 + k * (k - 1) // 2 + j
            loads[b].wait()
            acc = acc - jnp.dot(
                panels[b], held[j], preferred_element_type=jnp.float32
            )
        loads[k].wait()
        held[k] = jnp.dot(
            panels[k], acc.astype(jnp.bfloat16), preferred_element_type=jnp.float32
        ).astype(jnp.bfloat16)
        stores.append(
            pltpu.make_async_copy(
                held.at[k], out.at[k * 512 : (k + 1) * 512], sems.at[10 + k]
            )
        )
        stores[-1].start()
    for store in stores:
        store.wait()


def cost(flops, moved):
    return pl.CostEstimate(flops=flops, bytes_accessed=moved, transcendentals=0)


def ring(count, shift):
    return [(i, (i + shift) % count) for i in range(count)]


def local(integrals, inverses, lower_blocks):
    rows, total = integrals.shape
    width = total // (NX * NY)
    bf16 = jnp.bfloat16
    late_width = width - EARLY

    first = pl.pallas_call(
        pack_first,
        out_shape=jax.ShapeDtypeStruct((NY, 9, 16, width), bf16),
        in_specs=[ANY] * 3,
        out_specs=VMEM,
        scratch_shapes=[pltpu.SemaphoreType.DMA((NX * NY + 2 * NY,))],
        cost_estimate=cost(0, 3 << 20),
    )(integrals.reshape(4, 16, total), inverses, lower_blocks)
    first = lax.all_to_all(first, "y", 0, 0, tiled=True)

    slabs = pl.pallas_call(
        pack_late,
        out_shape=[jax.ShapeDtypeStruct((NY, rows, late_width), bf16)] * NX,
        in_specs=[ANY],
        out_specs=[VMEM] * NX,
        scratch_shapes=[pltpu.SemaphoreType.DMA((NX * NY,))],
        cost_estimate=cost(0, 3 << 20),
    )(integrals)
    moved = {0: slabs[0]}
    for s in (1, 3, 2):
        moved[s] = lax.ppermute(slabs[s], "x", ring(NX, s))
    late = jnp.stack([moved[s] for s in range(NX)], axis=1)
    late = lax.all_to_all(late, "y", 0, 0, tiled=True)

    own = {0: first[:, 4:9]}
    for s in (1, 3, 2):
        own[s] = lax.ppermute(own[0], "x", ring(NX, s))
    other = {s: lax.ppermute(own[s], "core", ring(2, 1)) for s in range(NX)}
    early = {
        s: first[:, 0:4, :, s * EARLY : (s + 1) * EARLY] for s in range(NX)
    }
    for s in (1, 3, 2):
        early[s] = lax.ppermute(early[s], "x", ring(NX, s))

    factor, columns = pl.pallas_call(
        assemble,
        out_shape=[
            jax.ShapeDtypeStruct((2, 5, 512, 512), bf16),
            jax.ShapeDtypeStruct((NX, NY, 4, 16, EARLY), bf16),
        ],
        in_specs=[VMEM] * (3 * NX),
        out_specs=[VMEM] * 2,
        compiler_params=pltpu.CompilerParams(vmem_limit_bytes=16 << 20),
        cost_estimate=cost(0, 11 << 20),
    )(*[d[s] for d in (own, other, early) for s in range(NX)])

    return pl.pallas_call(
        solve,
        out_shape=jax.ShapeDtypeStruct((4 * 512, width), bf16),
        in_specs=[ANY, VMEM, VMEM],
        out_specs=ANY,
        scratch_shapes=[
            pltpu.VMEM((10, 512, 512), bf16),
            pltpu.VMEM((4, 512, width), bf16),
            pltpu.SemaphoreType.DMA((14,)),
        ],
        compiler_params=pltpu.CompilerParams(vmem_limit_bytes=16 << 20),
        cost_estimate=cost(20 * 512**3, 9 << 20),
    )(factor.reshape(10, 512, 512), columns, late)


def solution(mesh):
    fine = Mesh(mesh.devices.reshape(8, 2, NX, NY), ("z", "core", "x", "y"))
    aux, grp = ("x", "y"), ("z", "core")
    placed = (P(aux, grp), P(None, aux, None), P(None, aux, None))
    return jax.shard_map(
        local,
        mesh=fine,
        in_specs=placed,
        out_specs=P(None, grp + aux),
        check_vma=False,
    )
```

```python
import jax
import jax.numpy as jnp
from jax import lax
from jax.experimental import pallas as pl
from jax.experimental.pallas import tpu as pltpu
from jax.sharding import Mesh, PartitionSpec as P

NX, NY = 4, 8
ANY = pl.BlockSpec(memory_space=pl.ANY)
VMEM = pl.BlockSpec(memory_space=pltpu.VMEM)


def pack_first(integrals, inverses, lower_blocks, first, half, sems):
    x, core = lax.axis_index("x"), lax.axis_index("core")
    width = integrals.shape[2] // (NX * NY)
    copies = []
    for y in range(NY):
        at = pl.multiple_of(x * (NY * width) + y * width, 128)
        copies.append(
            pltpu.make_async_copy(
                integrals.at[:, :, pl.ds(at, width)], first.at[y, 0:4], sems.at[y]
            )
        )
    for copy in copies:
        copy.start()

    @pl.when(core == 0)
    def _():
        half[0:4] = inverses[...]
        half[4] = lower_blocks[0]

    @pl.when(core == 1)
    def _():
        half[...] = lower_blocks[1:6]

    for y in range(NY):
        first[y, 4:9] = half[...]
    for copy in copies:
        copy.wait()


def pack_late(integrals, s1, s2, s3, sems):
    x = lax.axis_index("x")
    width = integrals.shape[1] // (NX * NY)
    copies = []
    for s, slab in ((1, s1), (3, s3), (2, s2)):
        for y in range(NY):
            at = pl.multiple_of(lax.rem(x + s, NX) * (NY * width) + y * width, 128)
            copies.append(
                pltpu.make_async_copy(
                    integrals.at[:, pl.ds(at, width)], slab.at[y], sems.at[len(copies)]
                )
            )
    for copy in copies:
        copy.start()
    for copy in copies:
        copy.wait()


def solve(*refs):
    own, other, first, late = refs[0:4], refs[4:8], refs[8], refs[9]
    out, factor, held, sems = refs[10:]
    x, core = lax.axis_index("x"), lax.axis_index("core")
    for s in range(NX):
        row = pl.multiple_of(lax.rem(x + NX - s, NX) * 128, 128)
        for pieces, half in ((own, core), (other, 1 - core)):
            for b in range(5):
                factor[half * 5 + b, pl.ds(row, 128), :] = pieces[s][:, b].reshape(
                    128, 512
                )
    stores = []
    for k in range(4):
        slot = lax.rem(x + NX - k, NX)
        acc = jnp.where(
            slot == 0,
            first[:, 0:4].reshape(512, 512),
            late[:, jnp.maximum(slot - 1, 0)].reshape(512, 512),
        ).astype(jnp.float32)
        for j in range(k):
            acc = acc - jnp.dot(
                factor[4 + k * (k - 1) // 2 + j],
                held[j],
                preferred_element_type=jnp.float32,
            )
        held[k] = jnp.dot(
            factor[k], acc.astype(jnp.bfloat16), preferred_element_type=jnp.float32
        ).astype(jnp.bfloat16)
        stores.append(
            pltpu.make_async_copy(
                held.at[k], out.at[k * 512 : (k + 1) * 512], sems.at[k]
            )
        )
        stores[-1].start()
    for store in stores:
        store.wait()


def cost(flops, moved):
    return pl.CostEstimate(flops=flops, bytes_accessed=moved, transcendentals=0)


def ring(count, shift):
    return [(i, (i + shift) % count) for i in range(count)]


def local(integrals, inverses, lower_blocks):
    rows, total = integrals.shape
    width = total // (NX * NY)
    bf16 = jnp.bfloat16

    first = pl.pallas_call(
        pack_first,
        out_shape=jax.ShapeDtypeStruct((NY, 9, 16, width), bf16),
        in_specs=[ANY, VMEM, VMEM],
        out_specs=VMEM,
        scratch_shapes=[
            pltpu.VMEM((5, 16, 512), bf16),
            pltpu.SemaphoreType.DMA((NY,)),
        ],
        cost_estimate=cost(0, 3 << 20),
    )(integrals.reshape(4, 16, total), inverses, lower_blocks)
    first = lax.all_to_all(first, "y", 0, 0, tiled=True)

    slabs = pl.pallas_call(
        pack_late,
        out_shape=[jax.ShapeDtypeStruct((NY, rows, width), bf16)] * 3,
        in_specs=[ANY],
        out_specs=[VMEM] * 3,
        scratch_shapes=[pltpu.SemaphoreType.DMA((3 * NY,))],
        cost_estimate=cost(0, 3 << 20),
    )(integrals)
    moved = {s: lax.ppermute(slabs[s - 1], "x", ring(NX, s)) for s in (1, 3, 2)}
    late = jnp.stack([moved[s] for s in (1, 2, 3)], axis=1)
    late = lax.all_to_all(late, "y", 0, 0, tiled=True)

    own = {0: first[:, 4:9]}
    for s in (1, 3, 2):
        own[s] = lax.ppermute(own[0], "x", ring(NX, s))
    other = {s: lax.ppermute(own[s], "core", ring(2, 1)) for s in range(NX)}

    return pl.pallas_call(
        solve,
        out_shape=jax.ShapeDtypeStruct((4 * 512, width), bf16),
        in_specs=[VMEM] * 10,
        out_specs=ANY,
        scratch_shapes=[
            pltpu.VMEM((10, 512, 512), bf16),
            pltpu.VMEM((4, 512, width), bf16),
            pltpu.SemaphoreType.DMA((4,)),
        ],
        compiler_params=pltpu.CompilerParams(vmem_limit_bytes=24 << 20),
        cost_estimate=cost(20 * 512**3, 9 << 20),
    )(
        *[own[s] for s in range(NX)],
        *[other[s] for s in range(NX)],
        first,
        late,
    )


def solution(mesh):
    fine = Mesh(mesh.devices.reshape(8, 2, NX, NY), ("z", "core", "x", "y"))
    aux, grp = ("x", "y"), ("z", "core")
    placed = (P(aux, grp), P(None, aux, None), P(None, aux, None))
    return jax.shard_map(
        local,
        mesh=fine,
        in_specs=placed,
        out_specs=P(None, grp + aux),
        check_vma=False,
    )
```

```python
import jax
import jax.numpy as jnp
from jax import lax
from jax.experimental import pallas as pl
from jax.experimental.pallas import tpu as pltpu
from jax.sharding import Mesh, PartitionSpec as P

NX, NY, NZ = 4, 8, 8
NAUX = NX * NY
AHEAD = 3
SPLIT = 1
UNITS = 5
GROUPS = ((0, 1, 7), (2, 6), (3, 5), (4,))
ANY = pl.BlockSpec(memory_space=pl.ANY)
VMEM = pl.BlockSpec(memory_space=pltpu.VMEM)


def assemble(*refs):
    own, swapped, factor = refs[:NZ], refs[NZ:-1], refs[-1]
    z, core = lax.axis_index("z"), lax.axis_index("core")
    other = {}
    for group, ref in zip(GROUPS, swapped):
        for at, d in enumerate(group):
            other[d] = (ref, at * UNITS)
    for d in range(NZ):
        unit = lax.rem(z + NZ - d, NZ) * UNITS
        for (ref, at), half in (((own[d], 0), core), (other[d], 1 - core)):
            row = pl.multiple_of(half * 256, 256)
            for i in range(UNITS):
                factor[unit + i, pl.ds(row, 256), :] = ref[at + i]


def product(panels, block, solved):
    left = jnp.concatenate([panels[4 * block + q] for q in range(4)], axis=1)
    out = jnp.dot(left, solved, preferred_element_type=jnp.float32)
    return jnp.concatenate(
        [
            out[half * 256 + aux * 8 : half * 256 + aux * 8 + 8]
            for aux in range(NAUX)
            for half in range(2)
        ],
        axis=0,
    )


def solve(factor, columns, out, panels, held, sems):
    below = [[4 + k * (k - 1) // 2 + j for j in range(k)] for k in range(4)]
    order = [b for k in range(4) for b in below[k] + [k]]
    loads = {}
    for b in order:
        units = pl.ds(4 * b, 4)
        loads[b] = pltpu.make_async_copy(
            factor.at[units], panels.at[units], sems.at[b]
        )

    def ready(b):
        loads[b].wait()
        ahead = order.index(b) + AHEAD
        if ahead < len(order):
            loads[order[ahead]].start()

    for b in order[:AHEAD]:
        loads[b].start()
    stores = []
    width = columns.shape[1] // SPLIT
    for k in range(4):
        rows = slice(k * 512, (k + 1) * 512)
        cuts = [slice(h * width, (h + 1) * width) for h in range(SPLIT)]
        acc = [columns[rows, cut].astype(jnp.float32) for cut in cuts]
        for j, b in enumerate(below[k]):
            ready(b)
            for h, cut in enumerate(cuts):
                acc[h] = acc[h] - product(panels, b, held[j, :, cut])
        ready(k)
        for h, cut in enumerate(cuts):
            held[k, :, cut] = product(panels, k, acc[h].astype(jnp.bfloat16)).astype(
                jnp.bfloat16
            )
        stores.append(pltpu.make_async_copy(held.at[k], out.at[rows], sems.at[10 + k]))
        stores[-1].start()
    for store in stores:
        store.wait()


def cost(flops, moved):
    return pl.CostEstimate(flops=flops, bytes_accessed=moved, transcendentals=0)


def ring(count, shift):
    return [(i, (i + shift) % count) for i in range(count)]


def local(integrals, inverses, lower_blocks):
    rows, total = integrals.shape
    width = total // NAUX
    bf16 = jnp.bfloat16

    blocks = jnp.concatenate([inverses, lower_blocks], axis=0)
    blocks = lax.dynamic_slice_in_dim(blocks, 8 * lax.axis_index("core"), 8, 1)
    units = blocks.reshape(10, 8, 4, 128).transpose(0, 2, 1, 3).reshape(40, 8, 128)
    units = lax.dynamic_slice_in_dim(units, UNITS * lax.axis_index("z"), UNITS, 0)
    piece = jnp.broadcast_to(units[None], (NAUX, UNITS, 8, 128))
    piece = lax.all_to_all(piece, ("x", "y"), 0, 0, tiled=True)

    sections = integrals.reshape(rows, NAUX, width).transpose(1, 0, 2)
    sections, piece = lax.optimization_barrier((sections, piece))
    columns = lax.all_to_all(sections, ("x", "y"), 0, 0, tiled=True)

    own = {0: piece.transpose(1, 0, 2, 3).reshape(UNITS, NAUX * 8, 128)}
    for d in range(1, 5):
        own[d] = lax.ppermute(own[d - 1], "z", ring(NZ, 1))
        if d < 4:
            own[-d % NZ] = lax.ppermute(own[(1 - d) % NZ], "z", ring(NZ, -1))
    swapped = []
    for group in GROUPS:
        held = jnp.concatenate([own[d] for d in group], axis=0)
        swapped.append(lax.ppermute(held, "core", ring(2, 1)))

    factor = pl.pallas_call(
        assemble,
        out_shape=jax.ShapeDtypeStruct((40, 512, 128), bf16),
        in_specs=[VMEM] * (NZ + len(GROUPS)),
        out_specs=VMEM,
        compiler_params=pltpu.CompilerParams(vmem_limit_bytes=16 << 20),
        cost_estimate=cost(0, 10 << 20),
    )(*[own[d] for d in range(NZ)], *swapped)

    return pl.pallas_call(
        solve,
        out_shape=jax.ShapeDtypeStruct((4 * 512, width), bf16),
        in_specs=[ANY, VMEM],
        out_specs=ANY,
        scratch_shapes=[
            pltpu.VMEM((40, 512, 128), bf16),
            pltpu.VMEM((4, 512, width), bf16),
            pltpu.SemaphoreType.DMA((14,)),
        ],
        compiler_params=pltpu.CompilerParams(vmem_limit_bytes=48 << 20),
        cost_estimate=cost(20 * 512**3, 9 << 20),
    )(factor, columns.reshape(4 * 512, width))


def solution(mesh):
    fine = Mesh(mesh.devices.reshape(NZ, 2, NX, NY), ("z", "core", "x", "y"))
    aux, grp = ("x", "y"), ("z", "core")
    placed = (P(aux, grp), P(None, aux, None), P(None, aux, None))
    return jax.shard_map(
        local,
        mesh=fine,
        in_specs=placed,
        out_specs=P(None, grp + aux),
        check_vma=False,
    )
```

```python
import jax
import jax.numpy as jnp
from jax import lax
from jax.experimental import pallas as pl
from jax.experimental.pallas import tpu as pltpu
from jax.sharding import Mesh, PartitionSpec as P

NX, NY, NZ = 4, 8, 8
NAUX = NX * NY
AHEAD = 3
SPLIT = 1
UNITS = 5
ANY = pl.BlockSpec(memory_space=pl.ANY)
VMEM = pl.BlockSpec(memory_space=pltpu.VMEM)


def assemble(*refs):
    mine, theirs, swapped, factor = refs[:5], refs[5:9], refs[9:13], refs[13]
    z, core = lax.axis_index("z"), lax.axis_index("core")
    along = 1 - 2 * core
    places = []
    for d in range(5):
        near, far = z - along * d, z + along * d
        places.append((mine[d], 0, near, core))
        if d < 4:
            places.append((theirs[d], 0, near, 1 - core))
        if d > 0:
            places.append((swapped[d - 1], 0, far, 1 - core))
        if 0 < d < 4:
            places.append((swapped[d - 1], UNITS, far, core))
    for ref, at, source, half in places:
        unit = lax.rem(source + NZ, NZ) * UNITS
        row = pl.multiple_of(half * 256, 256)
        for i in range(UNITS):
            factor[unit + i, pl.ds(row, 256), :] = ref[at + i]


def product(panels, block, solved):
    left = jnp.concatenate([panels[4 * block + q] for q in range(4)], axis=1)
    out = jnp.dot(left, solved, preferred_element_type=jnp.float32)
    return jnp.concatenate(
        [
            out[half * 256 + aux * 8 : half * 256 + aux * 8 + 8]
            for aux in range(NAUX)
            for half in range(2)
        ],
        axis=0,
    )


def solve(factor, columns, out, panels, held, sems):
    below = [[4 + k * (k - 1) // 2 + j for j in range(k)] for k in range(4)]
    order = [b for k in range(4) for b in below[k] + [k]]
    loads = {}
    for b in order:
        units = pl.ds(4 * b, 4)
        loads[b] = pltpu.make_async_copy(
            factor.at[units], panels.at[units], sems.at[b]
        )

    def ready(b):
        loads[b].wait()
        ahead = order.index(b) + AHEAD
        if ahead < len(order):
            loads[order[ahead]].start()

    for b in order[:AHEAD]:
        loads[b].start()
    stores = []
    width = columns.shape[1] // SPLIT
    for k in range(4):
        rows = slice(k * 512, (k + 1) * 512)
        cuts = [slice(h * width, (h + 1) * width) for h in range(SPLIT)]
        acc = [columns[rows, cut].astype(jnp.float32) for cut in cuts]
        for j, b in enumerate(below[k]):
            ready(b)
            for h, cut in enumerate(cuts):
                acc[h] = acc[h] - product(panels, b, held[j, :, cut])
        ready(k)
        for h, cut in enumerate(cuts):
            held[k, :, cut] = product(panels, k, acc[h].astype(jnp.bfloat16)).astype(
                jnp.bfloat16
            )
        stores.append(pltpu.make_async_copy(held.at[k], out.at[rows], sems.at[10 + k]))
        stores[-1].start()
    for store in stores:
        store.wait()


def cost(flops, moved):
    return pl.CostEstimate(flops=flops, bytes_accessed=moved, transcendentals=0)


def ring(count, shift):
    return [(i, (i + shift) % count) for i in range(count)]


def local(integrals, inverses, lower_blocks):
    rows, total = integrals.shape
    width = total // NAUX
    bf16 = jnp.bfloat16

    blocks = jnp.concatenate([inverses, lower_blocks], axis=0)
    blocks = lax.dynamic_slice_in_dim(blocks, 8 * lax.axis_index("core"), 8, 1)
    units = blocks.reshape(10, 8, 4, 128).transpose(0, 2, 1, 3).reshape(40, 8, 128)
    units = lax.dynamic_slice_in_dim(units, UNITS * lax.axis_index("z"), UNITS, 0)
    piece = jnp.broadcast_to(units[None], (NAUX, UNITS, 8, 128))
    piece = lax.all_to_all(piece, ("x", "y"), 0, 0, tiled=True)

    sections = integrals.reshape(rows, NAUX, width).transpose(1, 0, 2)
    sections, piece = lax.optimization_barrier((sections, piece))
    columns = lax.all_to_all(sections, ("x", "y"), 0, 0, tiled=True)

    def swap(value):
        return lax.ppermute(value, "core", ring(2, 1))

    def pass_on(value):
        up = [(2 * z, 2 * ((z + 1) % NZ)) for z in range(NZ)]
        down = [(2 * z + 1, 2 * ((z - 1) % NZ) + 1) for z in range(NZ)]
        return lax.ppermute(value, ("z", "core"), up + down)

    mine = [piece.transpose(1, 0, 2, 3).reshape(UNITS, NAUX * 8, 128)]
    theirs = [swap(mine[0])]
    swapped = []
    for d in range(1, 5):
        mine.append(pass_on(mine[-1]))
        if d < 4:
            theirs.append(pass_on(theirs[-1]))
            swapped.append(swap(jnp.concatenate([mine[d], theirs[d]], axis=0)))
    swapped.append(swap(mine[4]))

    factor = pl.pallas_call(
        assemble,
        out_shape=jax.ShapeDtypeStruct((40, 512, 128), bf16),
        in_specs=[VMEM] * 13,
        out_specs=VMEM,
        compiler_params=pltpu.CompilerParams(vmem_limit_bytes=16 << 20),
        cost_estimate=cost(0, 10 << 20),
    )(*mine, *theirs, *swapped)

    return pl.pallas_call(
        solve,
        out_shape=jax.ShapeDtypeStruct((4 * 512, width), bf16),
        in_specs=[ANY, VMEM],
        out_specs=ANY,
        scratch_shapes=[
            pltpu.VMEM((40, 512, 128), bf16),
            pltpu.VMEM((4, 512, width), bf16),
            pltpu.SemaphoreType.DMA((14,)),
        ],
        compiler_params=pltpu.CompilerParams(vmem_limit_bytes=48 << 20),
        cost_estimate=cost(20 * 512**3, 9 << 20),
    )(factor, columns.reshape(4 * 512, width))


def solution(mesh):
    fine = Mesh(mesh.devices.reshape(NZ, 2, NX, NY), ("z", "core", "x", "y"))
    aux, grp = ("x", "y"), ("z", "core")
    placed = (P(aux, grp), P(None, aux, None), P(None, aux, None))
    return jax.shard_map(
        local,
        mesh=fine,
        in_specs=placed,
        out_specs=P(None, grp + aux),
        check_vma=False,
    )
```

```python
import jax
import jax.numpy as jnp
from jax import lax
from jax.experimental import pallas as pl
from jax.experimental.pallas import tpu as pltpu
from jax.sharding import Mesh, PartitionSpec as P

NX, NY, NZ = 4, 8, 8
NAUX = NX * NY
AHEAD = 3
SPLIT = 1
UNITS = 5
ANY = pl.BlockSpec(memory_space=pl.ANY)
VMEM = pl.BlockSpec(memory_space=pltpu.VMEM)


def assemble(*refs):
    mine, theirs, swapped, factor = refs[:5], refs[5:9], refs[9:13], refs[13]
    z, core = lax.axis_index("z"), lax.axis_index("core")
    along = 1 - 2 * core
    places = []
    for d in range(5):
        near, far = z - along * d, z + along * d
        places.append((mine[d], 0, near, core))
        if d < 4:
            places.append((theirs[d], 0, near, 1 - core))
        if d > 0:
            places.append((swapped[d - 1], 0, far, 1 - core))
        if 0 < d < 4:
            places.append((swapped[d - 1], UNITS, far, core))
    for ref, at, source, half in places:
        unit = lax.rem(source + NZ, NZ) * UNITS
        row = pl.multiple_of(half * 256, 256)
        for i in range(UNITS):
            factor[unit + i, pl.ds(row, 256), :] = ref[at + i]


def product(panels, block, solved):
    left = jnp.concatenate([panels[4 * block + q] for q in range(4)], axis=1)
    out = jnp.dot(left, solved, preferred_element_type=jnp.float32)
    return jnp.concatenate(
        [
            out[half * 256 + aux * 8 : half * 256 + aux * 8 + 8]
            for aux in range(NAUX)
            for half in range(2)
        ],
        axis=0,
    )


def solve(factor, columns, out, panels, held, sems):
    below = [[4 + k * (k - 1) // 2 + j for j in range(k)] for k in range(4)]
    order = [b for k in range(4) for b in below[k] + [k]]
    loads = {}
    for b in order:
        units = pl.ds(4 * b, 4)
        loads[b] = pltpu.make_async_copy(
            factor.at[units], panels.at[units], sems.at[b]
        )

    def ready(b):
        loads[b].wait()
        ahead = order.index(b) + AHEAD
        if ahead < len(order):
            loads[order[ahead]].start()

    for b in order[:AHEAD]:
        loads[b].start()
    stores = []
    width = columns.shape[1] // SPLIT
    for k in range(4):
        rows = slice(k * 512, (k + 1) * 512)
        cuts = [slice(h * width, (h + 1) * width) for h in range(SPLIT)]
        acc = [columns[rows, cut].astype(jnp.float32) for cut in cuts]
        for j, b in enumerate(below[k]):
            ready(b)
            for h, cut in enumerate(cuts):
                acc[h] = acc[h] - product(panels, b, held[j, :, cut])
        ready(k)
        for h, cut in enumerate(cuts):
            held[k, :, cut] = product(panels, k, acc[h].astype(jnp.bfloat16)).astype(
                jnp.bfloat16
            )
        stores.append(pltpu.make_async_copy(held.at[k], out.at[rows], sems.at[10 + k]))
        stores[-1].start()
    for store in stores:
        store.wait()


def cost(flops, moved):
    return pl.CostEstimate(flops=flops, bytes_accessed=moved, transcendentals=0)


def ring(count, shift):
    return [(i, (i + shift) % count) for i in range(count)]


def local(integrals, inverses, lower_blocks):
    rows, total = integrals.shape
    width = total // NAUX
    bf16 = jnp.bfloat16

    blocks = jnp.concatenate([inverses, lower_blocks], axis=0)
    blocks = lax.dynamic_slice_in_dim(blocks, 8 * lax.axis_index("core"), 8, 1)
    units = blocks.reshape(10, 8, 4, 128).transpose(0, 2, 1, 3).reshape(40, 8, 128)
    units = lax.dynamic_slice_in_dim(units, UNITS * lax.axis_index("z"), UNITS, 0)
    piece = jnp.broadcast_to(units[None], (NAUX, UNITS, 8, 128))
    piece = lax.all_to_all(piece, ("x", "y"), 0, 0, tiled=True)

    sections = integrals.reshape(rows, NAUX, width).transpose(1, 0, 2)
    sections, piece = lax.optimization_barrier((sections, piece))
    columns = lax.all_to_all(sections, ("x", "y"), 0, 0, tiled=True)

    def swap(value):
        return lax.ppermute(value, "core", ring(2, 1))

    def pass_on(value):
        up = [(2 * z, 2 * ((z + 1) % NZ)) for z in range(NZ)]
        down = [(2 * z + 1, 2 * ((z - 1) % NZ) + 1) for z in range(NZ)]
        return lax.ppermute(value, ("z", "core"), up + down)

    mine = [piece.transpose(1, 0, 2, 3).reshape(UNITS, NAUX * 8, 128)]
    theirs = [swap(mine[0])]
    for d in range(1, 4):
        mine.append(pass_on(mine[-1]))
        theirs.append(pass_on(theirs[-1]))
    pairs = [jnp.concatenate([mine[d], theirs[d]], axis=0) for d in range(1, 4)]
    pairs[0], pairs[1], mine[3] = lax.optimization_barrier(
        (pairs[0], pairs[1], mine[3])
    )
    mine.append(pass_on(mine[3]))
    swapped = [swap(pair) for pair in pairs] + [swap(mine[4])]

    factor = pl.pallas_call(
        assemble,
        out_shape=jax.ShapeDtypeStruct((40, 512, 128), bf16),
        in_specs=[VMEM] * 13,
        out_specs=VMEM,
        compiler_params=pltpu.CompilerParams(vmem_limit_bytes=16 << 20),
        cost_estimate=cost(0, 10 << 20),
    )(*mine, *theirs, *swapped)

    return pl.pallas_call(
        solve,
        out_shape=jax.ShapeDtypeStruct((4 * 512, width), bf16),
        in_specs=[ANY, VMEM],
        out_specs=ANY,
        scratch_shapes=[
            pltpu.VMEM((40, 512, 128), bf16),
            pltpu.VMEM((4, 512, width), bf16),
            pltpu.SemaphoreType.DMA((14,)),
        ],
        compiler_params=pltpu.CompilerParams(vmem_limit_bytes=48 << 20),
        cost_estimate=cost(20 * 512**3, 9 << 20),
    )(factor, columns.reshape(4 * 512, width))


def solution(mesh):
    fine = Mesh(mesh.devices.reshape(NZ, 2, NX, NY), ("z", "core", "x", "y"))
    aux, grp = ("x", "y"), ("z", "core")
    placed = (P(aux, grp), P(None, aux, None), P(None, aux, None))
    return jax.shard_map(
        local,
        mesh=fine,
        in_specs=placed,
        out_specs=P(None, grp + aux),
        check_vma=False,
    )
```

```python
import jax
import jax.numpy as jnp
from jax import lax
from jax.experimental import pallas as pl
from jax.experimental.pallas import tpu as pltpu
from jax.sharding import Mesh, PartitionSpec as P

NX, NY, NZ = 4, 8, 8
NAUX = NX * NY
AHEAD = 8
SPLIT = 1
FIRST = (0, 4)
UNITS = 5
ANY = pl.BlockSpec(memory_space=pl.ANY)
VMEM = pl.BlockSpec(memory_space=pltpu.VMEM)


def assemble(*refs):
    mine, theirs, swapped = refs[:5], refs[5:9], refs[9:13]
    factor, head = refs[13:]
    z, core = lax.axis_index("z"), lax.axis_index("core")
    along = 1 - 2 * core
    places = []
    for d in range(5):
        near, far = z - along * d, z + along * d
        places.append((mine[d], 0, near, core))
        if d < 4:
            places.append((theirs[d], 0, near, 1 - core))
        if d > 0:
            places.append((swapped[d - 1], 0, far, 1 - core))
        if 0 < d < 4:
            places.append((swapped[d - 1], UNITS, far, core))
    for ref, at, source, half in places:
        unit = lax.rem(source + NZ, NZ) * UNITS
        row = pl.multiple_of(half * 256, 256)
        for i in range(UNITS):
            factor[unit + i, pl.ds(row, 256), :] = ref[at + i]
    for at, block in enumerate(FIRST):
        head[4 * at : 4 * at + 4] = factor[4 * block : 4 * block + 4]


def product(panels, block, solved):
    left = jnp.concatenate([panels[4 * block + q] for q in range(4)], axis=1)
    out = jnp.dot(left, solved, preferred_element_type=jnp.float32)
    return jnp.concatenate(
        [
            out[half * 256 + aux * 8 : half * 256 + aux * 8 + 8]
            for aux in range(NAUX)
            for half in range(2)
        ],
        axis=0,
    )


def solve(factor, head, columns, out, panels, held, sems):
    below = [[4 + k * (k - 1) // 2 + j for j in range(k)] for k in range(4)]
    order = [b for k in range(4) for b in below[k] + [k] if b not in FIRST]
    loads = {}
    for b in order:
        units = pl.ds(4 * b, 4)
        loads[b] = pltpu.make_async_copy(
            factor.at[units], panels.at[units], sems.at[b]
        )

    def ready(b):
        if b in FIRST:
            return head, FIRST.index(b)
        loads[b].wait()
        ahead = order.index(b) + AHEAD
        if ahead < len(order):
            loads[order[ahead]].start()
        return panels, b

    for b in order[:AHEAD]:
        loads[b].start()
    stores = []
    width = columns.shape[1] // SPLIT
    for k in range(4):
        rows = slice(k * 512, (k + 1) * 512)
        cuts = [slice(h * width, (h + 1) * width) for h in range(SPLIT)]
        acc = [columns[rows, cut].astype(jnp.float32) for cut in cuts]
        for j, b in enumerate(below[k]):
            left = ready(b)
            for h, cut in enumerate(cuts):
                acc[h] = acc[h] - product(*left, held[j, :, cut])
        left = ready(k)
        for h, cut in enumerate(cuts):
            held[k, :, cut] = product(*left, acc[h].astype(jnp.bfloat16)).astype(
                jnp.bfloat16
            )
        stores.append(pltpu.make_async_copy(held.at[k], out.at[rows], sems.at[10 + k]))
        stores[-1].start()
    for store in stores:
        store.wait()


def cost(flops, moved):
    return pl.CostEstimate(flops=flops, bytes_accessed=moved, transcendentals=0)


def ring(count, shift):
    return [(i, (i + shift) % count) for i in range(count)]


def local(integrals, inverses, lower_blocks):
    rows, total = integrals.shape
    width = total // NAUX
    bf16 = jnp.bfloat16

    blocks = jnp.concatenate([inverses, lower_blocks], axis=0)
    blocks = lax.dynamic_slice_in_dim(blocks, 8 * lax.axis_index("core"), 8, 1)
    units = blocks.reshape(10, 8, 4, 128).transpose(0, 2, 1, 3).reshape(40, 8, 128)
    units = lax.dynamic_slice_in_dim(units, UNITS * lax.axis_index("z"), UNITS, 0)
    piece = jnp.broadcast_to(units[None], (NAUX, UNITS, 8, 128))
    piece = lax.all_to_all(piece, ("x", "y"), 0, 0, tiled=True)

    sections = integrals.reshape(rows, NAUX, width).transpose(1, 0, 2)
    sections, piece = lax.optimization_barrier((sections, piece))
    columns = lax.all_to_all(sections, ("x", "y"), 0, 0, tiled=True)

    def swap(value):
        return lax.ppermute(value, "core", ring(2, 1))

    def pass_on(value):
        up = [(2 * z, 2 * ((z + 1) % NZ)) for z in range(NZ)]
        down = [(2 * z + 1, 2 * ((z - 1) % NZ) + 1) for z in range(NZ)]
        return lax.ppermute(value, ("z", "core"), up + down)

    mine = [piece.transpose(1, 0, 2, 3).reshape(UNITS, NAUX * 8, 128)]
    theirs = [swap(mine[0])]
    for d in range(1, 4):
        mine.append(pass_on(mine[-1]))
        theirs.append(pass_on(theirs[-1]))
    pairs = [jnp.concatenate([mine[d], theirs[d]], axis=0) for d in range(1, 4)]
    pairs[0], pairs[1], mine[3] = lax.optimization_barrier(
        (pairs[0], pairs[1], mine[3])
    )
    mine.append(pass_on(mine[3]))
    swapped = [swap(pair) for pair in pairs] + [swap(mine[4])]

    factor, head = pl.pallas_call(
        assemble,
        out_shape=[
            jax.ShapeDtypeStruct((40, 512, 128), bf16),
            jax.ShapeDtypeStruct((4 * len(FIRST), 512, 128), bf16),
        ],
        in_specs=[VMEM] * 13,
        out_specs=[VMEM] * 2,
        compiler_params=pltpu.CompilerParams(vmem_limit_bytes=16 << 20),
        cost_estimate=cost(0, 10 << 20),
    )(*mine, *theirs, *swapped)

    return pl.pallas_call(
        solve,
        out_shape=jax.ShapeDtypeStruct((4 * 512, width), bf16),
        in_specs=[ANY, VMEM, VMEM],
        out_specs=ANY,
        scratch_shapes=[
            pltpu.VMEM((40, 512, 128), bf16),
            pltpu.VMEM((4, 512, width), bf16),
            pltpu.SemaphoreType.DMA((14,)),
        ],
        compiler_params=pltpu.CompilerParams(vmem_limit_bytes=48 << 20),
        cost_estimate=cost(20 * 512**3, 9 << 20),
    )(factor, head, columns.reshape(4 * 512, width))


def solution(mesh):
    fine = Mesh(mesh.devices.reshape(NZ, 2, NX, NY), ("z", "core", "x", "y"))
    aux, grp = ("x", "y"), ("z", "core")
    placed = (P(aux, grp), P(None, aux, None), P(None, aux, None))
    return jax.shard_map(
        local,
        mesh=fine,
        in_specs=placed,
        out_specs=P(None, grp + aux),
        check_vma=False,
    )
```
